256 devices in a mesh: section: 4 (over x), dp: 16 (over z, core), mp: 4 (over y).
Axes of the slice: x: 4, y: 4, z: 8, core: 2. Of those that a mesh axis runs over, the one named last changes fastest.
Arguments:
- teacher_feats: bfloat16 [8, 2048, 8192], P('section', 'dp', 'mp')
- layer_map: int32 [4], replicated, may hold values from 0 to 7
- student_in: bfloat16 [4, 2048, 2048], P('section', 'dp', 'mp')
- layer_weight: bfloat16 [4, 2048, 2048], P('section', 'dp', 'mp'), may hold values from -0.125 to 0.125
- proj_weight: bfloat16 [4, 2048, 8192], P('section', None, 'mp'), may hold values from -0.0625 to 0.0625
- token_weight: float32 [2048], P('dp'), may hold values from 256 to 2048
Outputs:
- grad_inputs: bfloat16 [4, 2048, 2048], P('section', 'dp', 'mp')
- grad_layer: float32 [4, 2048, 2048], P('section', 'dp', 'mp')
- grad_proj: float32 [4, 2048, 8192], P('section', 'dp', 'mp')
The draws below stay inside these ranges and needn't reach their ends.
All inputs are finite; a program needn't handle non-finite values.
Results may differ from the reference program's by a relative error of at most 0.023.
Values may be sent and summed in bfloat16 or wider, within the bound.
No kernel may reach another device: no remote copies, remote signals or barrier semaphores. Data moves between devices by JAX's collectives and lax.ppermute only.
A program may use at most 128 MiB of HBM per device.

```python
import math
import jax
import jax.numpy as jnp
from jax import lax

D = 2048
DT = 8192
TOK_DEV = 128
TOKENS = 2048
TLAYERS = 8
SLAYERS = 4
N_SECTION = 4
N_DP = 16


def rough_field(key, lead, rows, cols, divisor):
    k_base, k_col, k_row = jax.random.split(key, 3)
    base = jax.random.normal(k_base, (lead, rows, cols), jnp.float32)
    rising = jnp.exp(jnp.arange(cols, dtype=jnp.float32) * (math.log(3.0) / cols))
    col_scale = jnp.exp(jax.random.uniform(k_col, (cols,), jnp.float32) * math.log(10.0)) * rising
    row_scale = jnp.exp(jax.random.uniform(k_row, (lead, rows, 1), jnp.float32) * math.log(10.0))
    return base * col_scale * row_scale / divisor


def draw_teacher_feats(key, part):
    key = jax.random.fold_in(key, 11)
    return rough_field(key, TLAYERS, TOKENS, DT, 8.0).astype(jnp.bfloat16)


def draw_student_in(key, part):
    key = jax.random.fold_in(key, 23)
    return rough_field(key, SLAYERS, TOKENS, D, 64.0).astype(jnp.bfloat16)


def place_ends(result, own_key, smallest, largest):
    longest = result.shape.index(max(result.shape))
    spots = []
    for shift in (0, 1):
        where = [jax.random.randint(jax.random.fold_in(own_key, axis), (), 0, length) for axis, length in enumerate(result.shape)]
        where[longest] = (where[longest] + shift) % result.shape[longest]
        spots.append(tuple(where))
    return result.at[spots[0]].set(smallest).at[spots[1]].set(largest)


def block_scale(key, extent, shards, least, top_value):
    def one(axis_at, parts):
        heights = jax.random.uniform(jax.random.fold_in(jax.random.fold_in(key, 6), axis_at), (parts,), jnp.float32, least / len(shards), top_value / len(shards))
        return jnp.repeat(jnp.exp(heights), extent[axis_at] // parts).reshape((-1,) + (1,) * (len(extent) - axis_at - 1))

    gain = one(*shards[0])
    for cut in shards[1:]:
        gain = gain * one(*cut)
    return gain


def centred(stream_key, shape, width, bound, cuts=(), held_as=jnp.bfloat16):
    entries = width * jax.random.normal(stream_key, shape, jnp.float32)
    if cuts:
        entries = entries * block_scale(stream_key, shape, cuts, -0.22, 0.18)
    return jnp.clip(entries, -bound, bound).astype(held_as)


def setup_inputs(seed: int = 0) -> dict:
    keys = jax.random.split(jax.random.key(seed), 7)
    teacher_feats = draw_teacher_feats(jax.random.fold_in(keys[6], 71), 0)
    layer_map = place_ends(jax.random.randint(keys[1], (SLAYERS,), 0, TLAYERS), jax.random.fold_in(keys[1], 1), 0, TLAYERS - 1).astype(jnp.int32)
    student_in = draw_student_in(jax.random.fold_in(keys[6], 71), 0)
    layer_weight = centred(keys[3], (SLAYERS, D, D), D ** -0.5, 0.125, ((0, 4), (1, 16), (2, 4)))
    proj_weight = centred(keys[4], (SLAYERS, D, DT), DT ** -0.5, 0.0625, ((0, 4), (2, 4)))
    token_weight = jnp.clip(jnp.exp(math.log(2048.0) - 2.0794415 * jax.random.uniform(keys[5], (TOKENS,), jnp.float32) ** block_scale(keys[5], (TOKENS,), ((0, 16),), -0.2, 0.2)), 256.0, 2048.0)
    return dict(teacher_feats=teacher_feats, layer_map=layer_map, student_in=student_in, layer_weight=layer_weight, proj_weight=proj_weight, token_weight=token_weight)


epsilon_sq = 1e-06

def block_sum(left, right):
    left_blocks = left.reshape(N_DP, TOK_DEV, left.shape[1])
    right_blocks = right.reshape(N_DP, TOK_DEV, right.shape[1])

    def step(acc, pair):
        part = jnp.dot(pair[0].T, pair[1], preferred_element_type=jnp.float32)
        rounded = lax.optimization_barrier(part.astype(jnp.bfloat16))
        return (acc + rounded.astype(jnp.float32), None)
    start = jnp.zeros((left.shape[1], right.shape[1]), jnp.float32)
    return lax.scan(step, start, (left_blocks, right_blocks))[0]

def reference(teacher_feats, layer_map, student_in, layer_weight, proj_weight, token_weight):
    incoming = jnp.zeros((TOKENS, D), jnp.float32)
    inputs_out = [None] * N_SECTION
    layer_out = [None] * N_SECTION
    proj_out = [None] * N_SECTION
    for section_id in reversed(range(N_SECTION)):
        hidden = student_in[section_id]
        weight = layer_weight[section_id]
        project = proj_weight[section_id]
        picked = lax.dynamic_index_in_dim(teacher_feats, layer_map[section_id].astype(jnp.int32), 0, keepdims=False)
        pre = jnp.dot(hidden, weight, preferred_element_type=jnp.float32)
        squash = jnp.tanh(pre)
        act = hidden.astype(jnp.float32) + squash
        slope = 1.0 - squash * squash
        proj = jnp.dot(picked, project.T, preferred_element_type=jnp.float32)
        sum_aa = lax.optimization_barrier(jnp.sum(act * act, axis=1))
        sum_qq = lax.optimization_barrier(jnp.sum(proj * proj, axis=1))
        sum_aq = lax.optimization_barrier(jnp.sum(act * proj, axis=1))
        inv_a = lax.rsqrt(sum_aa + epsilon_sq)
        inv_q = lax.rsqrt(sum_qq + epsilon_sq)
        cgrad = (-(token_weight * inv_a * inv_q))[:, None] * proj + (token_weight * sum_aq * inv_a ** 3 * inv_q)[:, None] * act
        qgrad = ((-(token_weight * inv_a * inv_q))[:, None] * act + (token_weight * sum_aq * inv_a * inv_q ** 3)[:, None] * proj).astype(jnp.bfloat16)
        total = cgrad + incoming
        sgate = (total * slope).astype(jnp.bfloat16)
        back = total + jnp.dot(sgate, weight.T, preferred_element_type=jnp.float32)
        incoming = back
        inputs_out[section_id] = back.astype(jnp.bfloat16)
        layer_out[section_id] = block_sum(hidden, sgate)
        proj_out[section_id] = block_sum(qgrad, picked)
    return (jnp.stack(inputs_out), jnp.stack(layer_out), jnp.stack(proj_out))
```

```python
import jax
import jax.numpy as jnp
from jax import lax
from jax.sharding import PartitionSpec as P

epsilon_sq = 1e-06
bf16 = jnp.bfloat16
f32 = jnp.float32


def shift(array, axis, by):
    n = lax.axis_size(axis)
    return lax.ppermute(array, axis, [(i, (i + by) % n) for i in range(n)])


def from_behind(array, axis, by):
    n = lax.axis_size(axis)
    return lax.ppermute(array, axis, [(i, i + by) for i in range(n) if 0 <= i + by < n])


def cross(array, bits):
    n = lax.axis_size("dp")
    return lax.ppermute(array, "dp", [(i, i ^ bits) for i in range(n)])


def to_pair(array, by):
    n = lax.axis_size("dp")
    return lax.ppermute(array, "dp", [(i, (i + 4 * by) % n) for i in range(n)])


def turn(blocks, start):
    n = blocks.shape[0]
    return lax.dynamic_slice_in_dim(jnp.concatenate([blocks, blocks], axis=0), start, n, axis=0)


def after(array, *earlier):
    return lax.optimization_barrier((array,) + earlier)[0]


def flip(array, axis, yes):
    return jnp.where(yes, jnp.flip(array, axis), array)


def pick(feats, layer_map):
    here = lax.axis_index("section")
    n = lax.axis_size("section")
    half = feats.shape[1] // 2

    def wanted(target):
        layer = lax.dynamic_index_in_dim(layer_map, target % n, keepdims=False)
        return layer // feats.shape[0], lax.dynamic_index_in_dim(
            feats, layer % feats.shape[0], 0, keepdims=False
        )

    _, across = wanted(here + 2)
    owner_next, to_next = wanted(here + 1)
    owner_back, to_back = wanted(here + n - 1)
    from_left = shift(across[:half], "section", 1)
    from_right = shift(across[half:], "section", -1)
    left_last = shift(to_next[half:], "section", 1)
    right_first = shift(to_back[:half], "section", -1)
    left_first = shift(jnp.where(owner_next == here, to_next[:half], from_left), "section", 1)
    right_last = shift(jnp.where(owner_back == here, to_back[half:], from_right), "section", -1)
    owner, own = wanted(here)
    gap = (owner - here + n) % n
    first = jnp.where(gap == 0, own[:half], jnp.where(gap == 1, right_first, left_first))
    last = jnp.where(gap == 0, own[half:], jnp.where(gap == 3, left_last, right_last))
    return jnp.concatenate([first, last], axis=0)


def on_device(teacher_feats, layer_map, student_in, layer_weight, proj_weight, token_weight):
    section_count = lax.axis_size("section")
    m = lax.axis_index("mp")
    dp = lax.axis_index("dp")
    pair, place, in_pair, core = dp // 4, dp % 4, dp // 2 % 2, dp % 2
    hidden = student_in[0]
    tokens, width = hidden.shape

    mine = layer_weight[0]
    mine = jnp.stack([mine, cross(mine, 2)])
    picked = pick(teacher_feats, layer_map)
    hiddens = [hidden] + [shift(hidden, "mp", -d) for d in (1, 2, 3)]
    mine = jnp.stack([mine] + [to_pair(mine, -d) for d in (1, 2, 3)])
    rows = jnp.stack([mine, cross(mine, 1)], axis=2)
    rows = flip(flip(rows, 2, core == 1), 1, in_pair == 1).reshape(4, width, width)
    rel_weight = turn(rows, (m - pair + 4) % 4)

    project = proj_weight[0].reshape(4, width, -1)
    order = (2, 1, 3, 0)
    partial = {}
    for d in order:
        block = lax.dynamic_index_in_dim(project, (m + d) % 4, 0, keepdims=False)
        partial[d] = jnp.einsum("te,ke->tk", picked, block, preferred_element_type=f32)
    proj = partial[0] + sum(shift(partial[d].astype(bf16), "mp", d).astype(f32) for d in (2, 1, 3))

    pre = jnp.dot(
        jnp.concatenate(hiddens, axis=1), rel_weight.reshape(4 * width, width), preferred_element_type=f32
    )
    squash = jnp.tanh(pre)
    act = hidden.astype(f32) + squash
    slope = 1.0 - squash * squash
    sums = jnp.stack([jnp.sum(act * act, axis=1), jnp.sum(proj * proj, axis=1), jnp.sum(act * proj, axis=1)])
    sums = sums + sum(shift(sums, "mp", d) for d in (2, 1, 3))
    sum_aa, sum_qq, sum_aq = sums[0], sums[1], sums[2]
    inv_a = lax.rsqrt(sum_aa + epsilon_sq)
    inv_q = lax.rsqrt(sum_qq + epsilon_sq)
    cgrad = (-(token_weight * inv_a * inv_q))[:, None] * proj + (
        token_weight * sum_aq * inv_a**3 * inv_q
    )[:, None] * act
    qgrad = (
        (-(token_weight * inv_a * inv_q))[:, None] * act
        + (token_weight * sum_aq * inv_a * inv_q**3)[:, None] * proj
    ).astype(bf16)

    total = cgrad
    spreads = []
    for step in range(section_count):
        sgate = (total * slope).astype(bf16)
        result = total
        came = []
        for d in order:
            spread = jnp.einsum("tn,kn->tk", sgate, rel_weight[d], preferred_element_type=f32)
            if d == 0:
                result = result + spread
                spreads.append(result)
            else:
                came.append(shift(spread.astype(bf16), "mp", d))
        result = (result + sum(x.astype(f32) for x in came)).astype(bf16)
        if step + 1 < section_count:
            total = cgrad + from_behind(result, "section", -1).astype(f32)

    all_picked = lax.all_gather(
        picked, "dp", axis=0, tiled=True, axis_index_groups=[list(range(c, 16, 2)) for c in (0, 1)]
    )
    qgrad = after(qgrad, spreads[0])
    qgrads = jnp.stack([qgrad] + [shift(qgrad, "mp", -d) for d in (1, 2, 3)])
    qgrads = turn(qgrads, (pair - m + 4) % 4).reshape(4, tokens, 2, width // 2).swapaxes(1, 2)
    keep = lax.dynamic_index_in_dim(qgrads, in_pair, 1, keepdims=False)
    give = lax.dynamic_index_in_dim(qgrads, 1 - in_pair, 1, keepdims=False)
    both = jnp.stack([keep, cross(after(give, spreads[1]), 2)], axis=1)
    both = after(both, spreads[2])
    columns = jnp.stack([both[0]] + [to_pair(both[-d], -d) for d in (1, 2, 3)])
    columns = flip(turn(columns, (4 - pair) % 4), 1, in_pair == 1).reshape(8 * tokens, 2 * tokens)
    whole = jnp.einsum("tk,te->ke", columns, all_picked, preferred_element_type=f32)
    whole = whole.reshape(2, tokens, -1)
    grad_proj = lax.dynamic_index_in_dim(whole, core, 0, keepdims=False) + cross(
        lax.dynamic_index_in_dim(whole, 1 - core, 0, keepdims=False), 1
    )

    saved = turn(jnp.stack(hiddens), (pair - m + 4) % 4)
    saved = saved.reshape(4, tokens, 4, tokens).transpose(2, 0, 1, 3)
    saved = after(saved, picked)
    lefts = [lax.dynamic_index_in_dim(saved, place, 0, keepdims=False)]
    lefts += [cross(lax.dynamic_index_in_dim(saved, place ^ x, 0, keepdims=False), x) for x in (2, 1, 3)]
    gates = jnp.stack([sgate, cross(sgate, 2)])
    gates = jnp.concatenate([gates, cross(gates, 1)]).reshape(4 * tokens, width)
    lefts = jnp.concatenate(lefts, axis=1)
    parts = [jnp.einsum("tk,tn->kn", lefts[d], gates, preferred_element_type=f32) for d in range(4)]
    grad_layer = parts[0] + sum(to_pair(parts[d].astype(bf16), d).astype(f32) for d in (2, 1, 3))
    return (result[None], grad_layer[None], grad_proj[None])


def solution(mesh):
    placed = (
        P("section", "dp", "mp"),
        P(),
        P("section", "dp", "mp"),
        P("section", "dp", "mp"),
        P("section", None, "mp"),
        P("dp"),
    )
    return jax.shard_map(
        on_device,
        mesh=mesh,
        in_specs=placed,
        out_specs=(P("section", "dp", "mp"), P("section", "dp", "mp"), P("section", "dp", "mp")),
        check_vma=False,
    )
```

```python
import jax
import jax.numpy as jnp
from jax import lax
from jax.experimental import pallas as pl
from jax.experimental.pallas import tpu as pltpu
from jax.sharding import PartitionSpec as P

epsilon_sq = 1e-06
bf16 = jnp.bfloat16
f32 = jnp.float32
TOK = 128
WIDE = 512


def shift(array, axis, by):
    n = lax.axis_size(axis)
    return lax.ppermute(array, axis, [(i, (i + by) % n) for i in range(n)])


def to_previous(array):
    n = lax.axis_size("section")
    return lax.ppermute(array, "section", [(i, i - 1) for i in range(1, n)])


def along_z():
    return [list(range(core, lax.axis_size("dp"), 2)) for core in (0, 1)]


def gather_z(array):
    return lax.all_gather(array, "dp", axis=0, axis_index_groups=along_z())


def sum_z(array):
    return lax.psum_scatter(array, "dp", scatter_dimension=0, tiled=True, axis_index_groups=along_z())


def cross(array, bits):
    n = lax.axis_size("dp")
    return lax.ppermute(array, "dp", [(i, i ^ bits) for i in range(n)])


def to_pair(array, by):
    n = lax.axis_size("dp")
    return lax.ppermute(array, "dp", [(i, (i + 4 * by) % n) for i in range(n)])


def after(array, *earlier):
    return lax.optimization_barrier((array,) + earlier)[0]


def call(body, outs, *args, scratch=(), flops=0, limit=12):
    scalars = pl.BlockSpec(memory_space=pltpu.SMEM)
    size = sum(a.size * a.dtype.itemsize for a in args)
    return pl.pallas_call(
        body,
        out_shape=[jax.ShapeDtypeStruct(shape, dtype) for shape, dtype in outs],
        in_specs=[scalars if a.dtype == jnp.int32 else pl.BlockSpec() for a in args],
        out_specs=[pl.BlockSpec()] * len(outs),
        scratch_shapes=list(scratch),
        compiler_params=pltpu.CompilerParams(vmem_limit_bytes=limit * 2**20),
        cost_estimate=pl.CostEstimate(flops=flops, bytes_accessed=size, transcendentals=0),
    )(*args)


def dot(a, b, over):
    return lax.dot_general(a, b, (((over[0],), (over[1],)), ((), ())), preferred_element_type=f32)


def places():
    m = lax.axis_index("mp")
    dp = lax.axis_index("dp")
    return m, dp // 4, dp % 4, dp // 2, dp % 2


def pre_body(h0, h1, h2, h3, mine, theirs, weight, act, slope):
    m, _, _, _, core = places()
    total = None
    for d, hidden in enumerate((h0, h1, h2, h3)):
        for i in range(4):
            r = 2 * lax.rem(m + d, 4) + i // 2

            @pl.when(core == i % 2)
            def _():
                weight[d, i * TOK : (i + 1) * TOK] = mine[r]

            @pl.when(core != i % 2)
            def _():
                weight[d, i * TOK : (i + 1) * TOK] = theirs[r]

        part = dot(hidden[...], weight[d], (1, 0))
        total = part if total is None else total + part
    squash = jnp.tanh(total)
    act[...] = h0[...].astype(f32) + squash
    slope[...] = 1.0 - squash * squash


def sums_body(own, c2, c1, c3, act, proj, sums):
    value = own[...] + c2[...].astype(f32) + c1[...].astype(f32) + c3[...].astype(f32)
    proj[...] = value
    side = act[...]
    lane = lax.broadcasted_iota(jnp.int32, (TOK, TOK), 1)
    columns = jnp.zeros((TOK, TOK), f32)
    for i, product in enumerate((side * side, value * value, side * value)):
        columns = jnp.where(lane == i, jnp.sum(product, axis=1, keepdims=True), columns)
    sums[...] = columns.T[:8]


def first_body(s0, s1, s2, s3, scale, act, proj, slope, weight, cgrad, qgrad, own, gate, p2, p1, p3):
    sums = s0[...] + s1[...] + s2[...] + s3[...]
    rows = jnp.concatenate([sums, jnp.broadcast_to(scale[...], (8, TOK)), jnp.zeros((TOK - 16, TOK), f32)], axis=0)
    columns = rows.T
    sum_aa, sum_qq, sum_aq, scales = columns[:, 0:1], columns[:, 1:2], columns[:, 2:3], columns[:, 8:9]
    inv_a = lax.rsqrt(sum_aa + epsilon_sq)
    inv_q = lax.rsqrt(sum_qq + epsilon_sq)
    both = -(scales * inv_a * inv_q)
    total = both * proj[...] + (scales * sum_aq * inv_a * inv_a * inv_a * inv_q) * act[...]
    cgrad[...] = total
    qgrad[...] = (both * act[...] + (scales * sum_aq * inv_a * inv_q * inv_q * inv_q) * proj[...]).astype(bf16)
    spread(total, slope, weight, own, gate, p2, p1, p3)


def step_body(incoming, cgrad, slope, weight, own, gate, p2, p1, p3):
    spread(cgrad[...] + incoming[...].astype(f32), slope, weight, own, gate, p2, p1, p3)


def spread(total, slope, weight, own, gate, p2, p1, p3):
    sgate = (total * slope[...]).astype(bf16)
    gate[...] = sgate
    for d, part in ((2, p2), (1, p1), (3, p3)):
        part[...] = dot(sgate, weight[d], (1, 1)).astype(bf16)
    own[...] = total + dot(sgate, weight[0], (1, 1))


def saved_body(h0, h1, h2, h3, s0, s1, s2, s3, held):
    m, pair, place, _, _ = places()
    for d, hidden in enumerate((h0, h1, h2, h3)):
        held[d] = hidden[...]
    for x, out in enumerate((s0, s1, s2, s3)):
        start = pl.multiple_of((place ^ x) * TOK, TOK)
        for by in range(4):
            d = lax.rem(pair + by - m + 4, 4)
            out[:, by * TOK : (by + 1) * TOK] = held[d, :, pl.ds(start, TOK)]


def split_body(q0, q1, q2, q3, keep, give, held):
    m, _, _, _, core = places()
    for d, value in enumerate((q0, q1, q2, q3)):
        held[d] = value[...]
    for chip in range(8):
        d = lax.rem(chip // 2 - m + 4, 4)
        for out, place in ((keep, core), (give, 1 - core)):
            start = pl.multiple_of(chip % 2 * 256 + place * TOK, TOK)
            out[:, chip * TOK : (chip + 1) * TOK] = held[d, :, pl.ds(start, TOK)]


def proj_grad_body(keep, came, picked, other, out):
    left = jnp.concatenate([keep[...], came[...]], axis=0)
    for tile in range(8):
        cut = slice(tile * 256, (tile + 1) * 256)
        right = jnp.concatenate([picked[:, cut], other[:, cut]], axis=0)
        out[:, cut] = dot(left, right, (0, 0)).astype(bf16)


def layer_grad_body(g0, g1, g2, g3, s0, s1, s2, s3, own, p1, p2, p3):
    gates = jnp.concatenate([g0[...], g1[...], g2[...], g3[...]], axis=0)
    for by, out in ((2, p2), (1, p1), (3, p3), (0, own)):
        cut = slice(by * TOK, (by + 1) * TOK)
        left = jnp.concatenate([s0[:, cut], s1[:, cut], s2[:, cut], s3[:, cut]], axis=0)
        out[...] = dot(left, gates, (0, 0)).astype(out.dtype)


def choose_body(layers, feats, across_first, across_last, own):
    here = lax.axis_index("section")
    half = TOK // 2
    far = feats.at[lax.rem(layers[lax.rem(here + 2, 4)], 2)]
    across_first[...] = far[:half]
    across_last[...] = far[half:]
    own[...] = feats[lax.rem(layers[here], 2)]


def merge_body(layers, feats, from_left, from_right, to_next, to_back):
    here = lax.axis_index("section")
    half = TOK // 2
    for out, target, came, through in (
        (to_next, lax.rem(here + 1, 4), from_left, slice(0, half)),
        (to_back, lax.rem(here + 3, 4), from_right, slice(half, TOK)),
    ):
        layer = layers[target]
        out[...] = feats[lax.rem(layer, 2)]

        @pl.when(lax.div(layer, 2) != here)
        def _():
            out[through] = came[...]


def picked_body(layers, own, left, right, out):
    here = lax.axis_index("section")
    half = TOK // 2
    gap = lax.rem(lax.div(layers[here], 2) - here + 4, 4)

    @pl.when(gap == 0)
    def _():
        out[...] = own[...]

    @pl.when(gap == 1)
    def _():
        out[...] = right[...]

    @pl.when(gap == 2)
    def _():
        out[:half] = left[:half]
        out[half:] = right[half:]

    @pl.when(gap == 3)
    def _():
        out[...] = left[...]


def on_device(teacher_feats, layer_map, student_in, layer_weight, proj_weight, token_weight):
    section_count = lax.axis_size("section")
    m = lax.axis_index("mp")
    hidden = student_in[0]
    block = ((TOK, WIDE), bf16)
    wide = ((TOK, WIDE), f32)
    held = [pltpu.VMEM((4, TOK, WIDE), bf16)]

    half = ((TOK // 2, 2048), bf16)
    rows = ((TOK, 2048), bf16)
    mine = gather_z(layer_weight[0])
    across_first, across_last, own = call(choose_body, [half, half, rows], layer_map, teacher_feats)
    from_left = shift(across_first, "section", 1)
    from_right = shift(across_last, "section", -1)
    to_next, to_back = call(merge_body, [rows, rows], layer_map, teacher_feats, from_left, from_right)
    left = shift(to_next, "section", 1)
    right = shift(to_back, "section", -1)
    start = after(hidden, to_next)
    hiddens = [hidden] + [shift(start, "mp", -d) for d in (1, 2, 3)]
    saved = call(saved_body, [block] * 4, *hiddens, scratch=held)
    (picked,) = call(picked_body, [rows], layer_map, after(own, *hiddens), left, right)

    project = proj_weight[0].reshape(4, WIDE, -1)
    partial = []
    for d in (2, 1, 3, 0):
        part = lax.dynamic_index_in_dim(project, (m + d) % 4, 0, keepdims=False)
        partial.append(jnp.einsum("te,ke->tk", picked, part, preferred_element_type=f32))
    own = partial[3]
    came = [shift(part.astype(bf16), "mp", d) for part, d in zip(partial, (2, 1, 3))]
    other_picked = cross(after(picked, own), 1)
    mine = after(mine, *came)
    theirs = cross(mine, 1)
    weight, act, slope = call(pre_body, [((4, WIDE, WIDE), bf16), wide, wide], *hiddens, mine, theirs, flops=3 * 10**8)
    saved = [saved[0]] + [cross(after(saved[x], own), x) for x in (1, 2, 3)]
    proj, sums = call(sums_body, [wide, ((8, TOK), f32)], own, *came, act)

    cgrad, qgrad, own, sgate, *parts = call(
        first_body,
        [wide, block, wide, block, block, block, block],
        after(sums, *saved, other_picked),
        *[shift(sums, "mp", d) for d in (2, 1, 3)],
        token_weight.reshape(1, TOK),
        act,
        proj,
        slope,
        weight,
        flops=3 * 10**8,
    )
    for step in range(section_count):
        if step > 0:
            own, sgate, *parts = call(
                step_body,
                [wide, block, block, block, block],
                incoming,
                cgrad,
                slope,
                weight,
                flops=3 * 10**8,
            )
        last = step + 1 == section_count
        if last:
            gates = [sgate, cross(sgate, 1), cross(sgate, 2)]
            gates.append(cross(gates[2], 1))
            layer_own, *layer_parts = call(
                layer_grad_body, [wide, block, block, block], *gates, *saved, flops=3 * 10**8
            )
            parts = [after(part, layer_own) for part in parts]
        came = [shift(part, "mp", d) for part, d in zip(parts, (2, 1, 3))]
        result = (own + sum(x.astype(f32) for x in came)).astype(bf16)
        if not last:
            incoming = to_previous(result)
        if step == 0:
            start = after(qgrad, came[0])
            qgrads = [qgrad] + [shift(start, "mp", -d) for d in (1, 2, 3)]
            keep, give = call(split_body, [((TOK, 1024), bf16)] * 2, after(qgrads[0], incoming), *qgrads[1:], scratch=held)
            products = call(
                proj_grad_body,
                [((8 * TOK, 2048), bf16)],
                keep,
                cross(give, 1),
                picked,
                other_picked,
                limit=24,
            )
            grad_proj = sum_z(products[0])

    grad_proj = after(grad_proj, layer_own).astype(f32)
    grad_layer = after(layer_own, grad_proj, result)
    grad_layer = grad_layer + sum(to_pair(part, d).astype(f32) for part, d in zip(layer_parts, (1, 2, 3)))
    return (result[None], grad_layer[None], grad_proj[None])


def solution(mesh):
    placed = (
        P("section", "dp", "mp"),
        P(),
        P("section", "dp", "mp"),
        P("section", "dp", "mp"),
        P("section", None, "mp"),
        P("dp"),
    )
    return jax.shard_map(
        on_device,
        mesh=mesh,
        in_specs=placed,
        out_specs=(P("section", "dp", "mp"), P("section", "dp", "mp"), P("section", "dp", "mp")),
        check_vma=False,
    )
```

```python
import jax
import jax.numpy as jnp
from jax import lax
from jax.experimental import pallas as pl
from jax.experimental.pallas import tpu as pltpu
from jax.sharding import PartitionSpec as P

epsilon_sq = 1e-06
bf16 = jnp.bfloat16
f32 = jnp.float32
TOK = 128
WIDE = 512


def shift(array, axis, by):
    n = lax.axis_size(axis)
    return lax.ppermute(array, axis, [(i, (i + by) % n) for i in range(n)])


def to_previous(array):
    n = lax.axis_size("section")
    return lax.ppermute(array, "section", [(i, i - 1) for i in range(1, n)])


def along_z():
    return [list(range(core, lax.axis_size("dp"), 2)) for core in (0, 1)]


def gather_z(array):
    return lax.all_gather(array, "dp", axis=0, axis_index_groups=along_z())


def sum_z(array):
    return lax.psum_scatter(array, "dp", scatter_dimension=0, tiled=True, axis_index_groups=along_z())


def cross(array, bits):
    n = lax.axis_size("dp")
    return lax.ppermute(array, "dp", [(i, i ^ bits) for i in range(n)])


def to_pair(array, by):
    n = lax.axis_size("dp")
    return lax.ppermute(array, "dp", [(i, (i + 4 * by) % n) for i in range(n)])


def after(array, *earlier):
    return lax.optimization_barrier((array,) + earlier)[0]


def call(body, outs, *args, scratch=(), flops=0, limit=12, far=0, far_outs=0):
    scalars = pl.BlockSpec(memory_space=pltpu.SMEM)
    size = sum(a.size * a.dtype.itemsize for a in args)
    return pl.pallas_call(
        body,
        out_shape=[jax.ShapeDtypeStruct(shape, dtype) for shape, dtype in outs],
        in_specs=[scalars if a.dtype == jnp.int32 else pl.BlockSpec() for a in args[: len(args) - far]]
        + [pl.BlockSpec(memory_space=pltpu.HBM)] * far,
        out_specs=[pl.BlockSpec(memory_space=pltpu.HBM) if far_outs else pl.BlockSpec()] * len(outs),
        scratch_shapes=list(scratch),
        compiler_params=pltpu.CompilerParams(vmem_limit_bytes=limit * 2**20),
        cost_estimate=pl.CostEstimate(flops=flops, bytes_accessed=size, transcendentals=0),
    )(*args)


def dot(a, b, over):
    return lax.dot_general(a, b, (((over[0],), (over[1],)), ((), ())), preferred_element_type=f32)


def places():
    m = lax.axis_index("mp")
    dp = lax.axis_index("dp")
    return m, dp // 4, dp % 4, dp // 2, dp % 2


def pre_body(h0, h1, h2, h3, mine, theirs, weight, act, slope):
    m, _, _, _, core = places()
    total = None
    for d, hidden in enumerate((h0, h1, h2, h3)):
        for i in range(4):
            r = 2 * lax.rem(m + d, 4) + i // 2

            @pl.when(core == i % 2)
            def _():
                weight[d, i * TOK : (i + 1) * TOK] = mine[r]

            @pl.when(core != i % 2)
            def _():
                weight[d, i * TOK : (i + 1) * TOK] = theirs[r]

        part = dot(hidden[...], weight[d], (1, 0))
        total = part if total is None else total + part
    squash = jnp.tanh(total)
    act[...] = h0[...].astype(f32) + squash
    slope[...] = 1.0 - squash * squash


def bring_body(weight, out, sem):
    copy = pltpu.make_async_copy(weight, out, sem)
    copy.start()
    copy.wait()


def bring(weight):
    return pl.pallas_call(
        bring_body,
        out_shape=jax.ShapeDtypeStruct(weight.shape, weight.dtype),
        in_specs=[pl.BlockSpec(memory_space=pltpu.HBM)],
        out_specs=pl.BlockSpec(memory_space=pltpu.VMEM),
        scratch_shapes=[pltpu.SemaphoreType.DMA],
        compiler_params=pltpu.CompilerParams(vmem_limit_bytes=2 * 2**20),
        cost_estimate=pl.CostEstimate(flops=0, bytes_accessed=weight.size * 4, transcendentals=0),
    )(weight)


def sums_body(own, c2, c1, c3, act, proj, sums):
    value = own[...] + c2[...].astype(f32) + c1[...].astype(f32) + c3[...].astype(f32)
    proj[...] = value
    side = act[...]
    lane = lax.broadcasted_iota(jnp.int32, (TOK, TOK), 1)
    columns = jnp.zeros((TOK, TOK), f32)
    for i, product in enumerate((side * side, value * value, side * value)):
        columns = jnp.where(lane == i, jnp.sum(product, axis=1, keepdims=True), columns)
    sums[...] = columns.T[:8]


def first_body(s0, s1, s2, s3, scale, act, proj, slope, weight, cgrad, qgrad, own, gate, p2, p1, p3):
    sums = s0[...] + s1[...] + s2[...] + s3[...]
    rows = jnp.concatenate([sums, jnp.broadcast_to(scale[...], (8, TOK)), jnp.zeros((TOK - 16, TOK), f32)], axis=0)
    columns = rows.T
    sum_aa, sum_qq, sum_aq, scales = columns[:, 0:1], columns[:, 1:2], columns[:, 2:3], columns[:, 8:9]
    inv_a = lax.rsqrt(sum_aa + epsilon_sq)
    inv_q = lax.rsqrt(sum_qq + epsilon_sq)
    both = -(scales * inv_a * inv_q)
    total = both * proj[...] + (scales * sum_aq * inv_a * inv_a * inv_a * inv_q) * act[...]
    cgrad[...] = total
    qgrad[...] = (both * act[...] + (scales * sum_aq * inv_a * inv_q * inv_q * inv_q) * proj[...]).astype(bf16)
    spread(total, slope, weight, own, gate, p2, p1, p3)


def step_body(incoming, cgrad, slope, weight, own, gate, p2, p1, p3):
    spread(cgrad[...] + incoming[...].astype(f32), slope, weight, own, gate, p2, p1, p3)


def spread(total, slope, weight, own, gate, p2, p1, p3):
    sgate = (total * slope[...]).astype(bf16)
    gate[...] = sgate
    for d, part in ((2, p2), (1, p1), (3, p3)):
        part[...] = dot(sgate, weight[d], (1, 1)).astype(bf16)
    own[...] = total + dot(sgate, weight[0], (1, 1))


def saved_body(h0, h1, h2, h3, s0, s1, s2, s3, held, sems):
    m, pair, place, _, _ = places()
    for d, hidden in enumerate((h0, h1, h2, h3)):
        held[d] = hidden[...]
    copies = []
    for x, out in enumerate((s0, s1, s2, s3)):
        start = pl.multiple_of((place ^ x) * TOK, TOK)
        for by in range(4):
            d = lax.rem(pair + by - m + 4, 4)
            cut = pl.ds(by * TOK, TOK)
            copies.append(
                pltpu.make_async_copy(held.at[d, :, pl.ds(start, TOK)], out.at[:, cut], sems.at[x, by])
            )
    for copy in copies:
        copy.start()
    for copy in copies:
        copy.wait()


def split_body(q0, q1, q2, q3, keep, give, held):
    m, _, _, _, core = places()
    for d, value in enumerate((q0, q1, q2, q3)):
        held[d] = value[...]
    for chip in range(8):
        d = lax.rem(chip // 2 - m + 4, 4)
        for out, place in ((keep, core), (give, 1 - core)):
            start = pl.multiple_of(chip % 2 * 256 + place * TOK, TOK)
            out[:, chip * TOK : (chip + 1) * TOK] = held[d, :, pl.ds(start, TOK)]


def proj_grad_body(keep, came, picked, other, out):
    left = jnp.concatenate([keep[...], came[...]], axis=0)
    for tile in range(8):
        cut = slice(tile * 256, (tile + 1) * 256)
        right = jnp.concatenate([picked[:, cut], other[:, cut]], axis=0)
        out[:, cut] = dot(left, right, (0, 0)).astype(bf16)


def layer_grad_body(g0, g1, g2, g3, f0, f1, f2, f3, own, p1, p2, p3, s0, s1, s2, s3, sems):
    copies = [
        pltpu.make_async_copy(source, target, sems.at[i])
        for i, (source, target) in enumerate(zip((f0, f1, f2, f3), (s0, s1, s2, s3)))
    ]
    for copy in copies:
        copy.start()
    for copy in copies:
        copy.wait()
    gates = jnp.concatenate([g0[...], g1[...], g2[...], g3[...]], axis=0)
    for by, out in ((2, p2), (1, p1), (3, p3), (0, own)):
        cut = slice(by * TOK, (by + 1) * TOK)
        left = jnp.concatenate([s0[:, cut], s1[:, cut], s2[:, cut], s3[:, cut]], axis=0)
        out[...] = dot(left, gates, (0, 0)).astype(out.dtype)


def choose_body(layers, feats, across_first, across_last, own):
    here = lax.axis_index("section")
    half = TOK // 2
    far = feats.at[lax.rem(layers[lax.rem(here + 2, 4)], 2)]
    across_first[...] = far[:half]
    across_last[...] = far[half:]
    own[...] = feats[lax.rem(layers[here], 2)]


def merge_body(layers, feats, from_left, from_right, to_next, to_back):
    here = lax.axis_index("section")
    half = TOK // 2
    for out, target, came, through in (
        (to_next, lax.rem(here + 1, 4), from_left, slice(0, half)),
        (to_back, lax.rem(here + 3, 4), from_right, slice(half, TOK)),
    ):
        layer = layers[target]
        out[...] = feats[lax.rem(layer, 2)]

        @pl.when(lax.div(layer, 2) != here)
        def _():
            out[through] = came[...]


def picked_body(layers, own, left, right, out):
    here = lax.axis_index("section")
    half = TOK // 2
    gap = lax.rem(lax.div(layers[here], 2) - here + 4, 4)

    @pl.when(gap == 0)
    def _():
        out[...] = own[...]

    @pl.when(gap == 1)
    def _():
        out[...] = right[...]

    @pl.when(gap == 2)
    def _():
        out[:half] = left[:half]
        out[half:] = right[half:]

    @pl.when(gap == 3)
    def _():
        out[...] = left[...]


def on_device(teacher_feats, layer_map, student_in, layer_weight, proj_weight, token_weight):
    section_count = lax.axis_size("section")
    m = lax.axis_index("mp")
    hidden = student_in[0]
    block = ((TOK, WIDE), bf16)
    wide = ((TOK, WIDE), f32)
    held = [pltpu.VMEM((4, TOK, WIDE), bf16)]

    half = ((TOK // 2, 2048), bf16)
    rows = ((TOK, 2048), bf16)
    mine = gather_z(layer_weight[0])
    across_first, across_last, own = call(choose_body, [half, half, rows], layer_map, teacher_feats, flops=2 * 10**10)
    from_left = shift(across_first, "section", 1)
    from_right = shift(across_last, "section", -1)
    to_next, to_back = call(merge_body, [rows, rows], layer_map, teacher_feats, from_left, from_right)
    left = shift(to_next, "section", 1)
    right = shift(to_back, "section", -1)
    start = after(hidden, to_next)
    hiddens = [hidden] + [shift(start, "mp", -d) for d in (1, 2, 3)]
    saved = call(
        saved_body, [block] * 4, *hiddens, scratch=[*held, pltpu.SemaphoreType.DMA((4, 4))], far_outs=1
    )
    weights = bring(after(proj_weight[0].reshape(4, WIDE, -1), to_back))
    own, weights = lax.optimization_barrier((own, weights))
    (picked,) = call(picked_body, [rows], layer_map, after(own, *hiddens), left, right)

    partial = []
    for d in (2, 1, 3, 0):
        part = lax.dynamic_index_in_dim(weights, (m + d) % 4, 0, keepdims=False)
        partial.append(jnp.einsum("te,ke->tk", picked, part, preferred_element_type=f32))
    own = partial[3]
    came = [shift(part.astype(bf16), "mp", d) for part, d in zip(partial, (2, 1, 3))]
    other_picked = cross(after(picked, own), 1)
    mine = after(mine, own, *came)
    theirs = cross(mine, 1)
    weight, act, slope = call(pre_body, [((4, WIDE, WIDE), bf16), wide, wide], *hiddens, mine, theirs, flops=3 * 10**8)
    saved = [saved[0]] + [cross(after(saved[x], own), x) for x in (1, 2, 3)]
    proj, sums = call(sums_body, [wide, ((8, TOK), f32)], own, *came, act)

    cgrad, qgrad, own, sgate, *parts = call(
        first_body,
        [wide, block, wide, block, block, block, block],
        after(sums, *saved, other_picked),
        *[shift(sums, "mp", d) for d in (2, 1, 3)],
        token_weight.reshape(1, TOK),
        act,
        proj,
        slope,
        weight,
        flops=3 * 10**8,
    )
    for step in range(section_count):
        if step > 0:
            own, sgate, *parts = call(
                step_body,
                [wide, block, block, block, block],
                incoming,
                cgrad,
                slope,
                weight,
                flops=3 * 10**8,
            )
        last = step + 1 == section_count
        if last:
            gates = [sgate, cross(sgate, 1), cross(sgate, 2)]
            gates.append(cross(gates[2], 1))
            layer_own, *layer_parts = call(
                layer_grad_body,
                [wide, block, block, block],
                *gates,
                *saved,
                flops=3 * 10**8,
                scratch=[pltpu.VMEM((TOK, WIDE), bf16)] * 4 + [pltpu.SemaphoreType.DMA((4,))],
                far=4,
            )
            parts = [after(part, layer_own) for part in parts]
        came = [shift(part, "mp", d) for part, d in zip(parts, (2, 1, 3))]
        result = (own + sum(x.astype(f32) for x in came)).astype(bf16)
        if not last:
            incoming = to_previous(result)
        if step == 0:
            start = after(qgrad, came[0])
            qgrads = [qgrad] + [shift(start, "mp", -d) for d in (1, 2, 3)]
            keep, give = call(split_body, [((TOK, 1024), bf16)] * 2, after(qgrads[0], incoming), *qgrads[1:], scratch=held)
            products = call(
                proj_grad_body,
                [((8 * TOK, 2048), bf16)],
                keep,
                cross(give, 1),
                picked,
                other_picked,
                limit=24,
            )
            grad_proj = sum_z(products[0])

    grad_proj = after(grad_proj, layer_own).astype(f32)
    layer_own, grad_proj, result = lax.optimization_barrier((layer_own, grad_proj, result))
    grad_layer = layer_own + sum(to_pair(part, d).astype(f32) for part, d in zip(layer_parts, (1, 2, 3)))
    return (result[None], grad_layer[None], grad_proj[None])


def solution(mesh):
    placed = (
        P("section", "dp", "mp"),
        P(),
        P("section", "dp", "mp"),
        P("section", "dp", "mp"),
        P("section", None, "mp"),
        P("dp"),
    )
    return jax.shard_map(
        on_device,
        mesh=mesh,
        in_specs=placed,
        out_specs=(P("section", "dp", "mp"), P("section", "dp", "mp"), P("section", "dp", "mp")),
        check_vma=False,
    )
```

```python
import jax
import jax.numpy as jnp
from jax import lax
from jax.experimental import pallas as pl
from jax.experimental.pallas import tpu as pltpu
from jax.sharding import PartitionSpec as P

epsilon_sq = 1e-06
bf16 = jnp.bfloat16
f32 = jnp.float32
TOK = 128
WIDE = 512


def shift(array, axis, by):
    n = lax.axis_size(axis)
    return lax.ppermute(array, axis, [(i, (i + by) % n) for i in range(n)])


def to_previous(array):
    n = lax.axis_size("section")
    return lax.ppermute(array, "section", [(i, i - 1) for i in range(1, n)])


def along_z():
    return [list(range(core, lax.axis_size("dp"), 2)) for core in (0, 1)]


def gather_z(array):
    return lax.all_gather(array, "dp", axis=0, axis_index_groups=along_z())


def sum_z(array):
    return lax.psum_scatter(array, "dp", scatter_dimension=0, tiled=True, axis_index_groups=along_z())


def cross(array, bits):
    n = lax.axis_size("dp")
    return lax.ppermute(array, "dp", [(i, i ^ bits) for i in range(n)])


def to_pair(array, by):
    n = lax.axis_size("dp")
    return lax.ppermute(array, "dp", [(i, (i + 4 * by) % n) for i in range(n)])


def after(array, *earlier):
    return lax.optimization_barrier((array,) + earlier)[0]


def call(body, outs, *args, scratch=(), flops=0, limit=12, far=0, far_outs=0):
    scalars = pl.BlockSpec(memory_space=pltpu.SMEM)
    size = sum(a.size * a.dtype.itemsize for a in args)
    return pl.pallas_call(
        body,
        out_shape=[jax.ShapeDtypeStruct(shape, dtype) for shape, dtype in outs],
        in_specs=[scalars if a.dtype == jnp.int32 else pl.BlockSpec() for a in args[: len(args) - far]]
        + [pl.BlockSpec(memory_space=pltpu.HBM)] * far,
        out_specs=[pl.BlockSpec(memory_space=pltpu.HBM) if far_outs else pl.BlockSpec()] * len(outs),
        scratch_shapes=list(scratch),
        compiler_params=pltpu.CompilerParams(vmem_limit_bytes=limit * 2**20),
        cost_estimate=pl.CostEstimate(flops=flops, bytes_accessed=size, transcendentals=0),
    )(*args)


def dot(a, b, over):
    return lax.dot_general(a, b, (((over[0],), (over[1],)), ((), ())), preferred_element_type=f32)


def places():
    m = lax.axis_index("mp")
    dp = lax.axis_index("dp")
    return m, dp // 4, dp % 4, dp // 2, dp % 2


def pre_body(h0, h1, h2, h3, mine, theirs, weight, act, slope):
    m, _, _, _, core = places()
    total = None
    for d, hidden in enumerate((h0, h1, h2, h3)):
        for i in range(4):
            r = 2 * lax.rem(m + d, 4) + i // 2

            @pl.when(core == i % 2)
            def _():
                weight[d, i * TOK : (i + 1) * TOK] = mine[r]

            @pl.when(core != i % 2)
            def _():
                weight[d, i * TOK : (i + 1) * TOK] = theirs[r]

        part = dot(hidden[...], weight[d], (1, 0))
        total = part if total is None else total + part
    squash = jnp.tanh(total)
    act[...] = h0[...].astype(f32) + squash
    slope[...] = 1.0 - squash * squash


def bring_body(weight, out, sem):
    copy = pltpu.make_async_copy(weight, out, sem)
    copy.start()
    copy.wait()


def bring(weight):
    return pl.pallas_call(
        bring_body,
        out_shape=jax.ShapeDtypeStruct(weight.shape, weight.dtype),
        in_specs=[pl.BlockSpec(memory_space=pltpu.HBM)],
        out_specs=pl.BlockSpec(memory_space=pltpu.VMEM),
        scratch_shapes=[pltpu.SemaphoreType.DMA],
        compiler_params=pltpu.CompilerParams(vmem_limit_bytes=2 * 2**20),
        cost_estimate=pl.CostEstimate(flops=0, bytes_accessed=weight.size * 4, transcendentals=0),
    )(weight)


def sums_body(own, c2, c1, c3, act, proj, sums):
    value = own[...] + c2[...].astype(f32) + c1[...].astype(f32) + c3[...].astype(f32)
    proj[...] = value
    side = act[...]
    lane = lax.broadcasted_iota(jnp.int32, (TOK, TOK), 1)
    columns = jnp.zeros((TOK, TOK), f32)
    for i, product in enumerate((side * side, value * value, side * value)):
        columns = jnp.where(lane == i, jnp.sum(product, axis=1, keepdims=True), columns)
    sums[...] = columns.T[:8]


def first_body(s0, s1, s2, s3, scale, act, proj, slope, weight, cgrad, qgrad, own, gate, p2, p1, p3):
    sums = s0[...] + s1[...] + s2[...] + s3[...]
    rows = jnp.concatenate([sums, jnp.broadcast_to(scale[...], (8, TOK)), jnp.zeros((TOK - 16, TOK), f32)], axis=0)
    columns = rows.T
    sum_aa, sum_qq, sum_aq, scales = columns[:, 0:1], columns[:, 1:2], columns[:, 2:3], columns[:, 8:9]
    inv_a = lax.rsqrt(sum_aa + epsilon_sq)
    inv_q = lax.rsqrt(sum_qq + epsilon_sq)
    both = -(scales * inv_a * inv_q)
    total = both * proj[...] + (scales * sum_aq * inv_a * inv_a * inv_a * inv_q) * act[...]
    cgrad[...] = total
    qgrad[...] = (both * act[...] + (scales * sum_aq * inv_a * inv_q * inv_q * inv_q) * proj[...]).astype(bf16)
    spread(total, slope, weight, own, gate, p2, p1, p3)


def step_body(incoming, cgrad, slope, weight, own, gate, p2, p1, p3):
    spread(cgrad[...] + incoming[...].astype(f32), slope, weight, own, gate, p2, p1, p3)


def spread(total, slope, weight, own, gate, p2, p1, p3):
    sgate = (total * slope[...]).astype(bf16)
    gate[...] = sgate
    for d, part in ((2, p2), (1, p1), (3, p3)):
        part[...] = dot(sgate, weight[d], (1, 1)).astype(bf16)
    own[...] = total + dot(sgate, weight[0], (1, 1))


def saved_body(h0, h1, h2, h3, s0, s1, s2, s3, held, sems):
    m, pair, place, _, _ = places()
    for d, hidden in enumerate((h0, h1, h2, h3)):
        held[d] = hidden[...]
    copies = []
    for x, out in enumerate((s0, s1, s2, s3)):
        start = pl.multiple_of((place ^ x) * TOK, TOK)
        for by in range(4):
            d = lax.rem(pair + by - m + 4, 4)
            cut = pl.ds(by * TOK, TOK)
            copies.append(
                pltpu.make_async_copy(held.at[d, :, pl.ds(start, TOK)], out.at[:, cut], sems.at[x, by])
            )
    for copy in copies:
        copy.start()
    for copy in copies:
        copy.wait()


def split_body(q0, q1, q2, q3, keep, give, held):
    m, _, _, _, core = places()
    for d, value in enumerate((q0, q1, q2, q3)):
        held[d] = value[...]
    for chip in range(8):
        d = lax.rem(chip // 2 - m + 4, 4)
        for out, place in ((keep, core), (give, 1 - core)):
            start = pl.multiple_of(chip % 2 * 256 + place * TOK, TOK)
            out[:, chip * TOK : (chip + 1) * TOK] = held[d, :, pl.ds(start, TOK)]


def proj_grad_body(keep, came, picked, other, out):
    left = jnp.concatenate([keep[...], came[...]], axis=0)
    for tile in range(8):
        cut = slice(tile * 256, (tile + 1) * 256)
        right = jnp.concatenate([picked[:, cut], other[:, cut]], axis=0)
        out[:, cut] = dot(left, right, (0, 0)).astype(bf16)


def layer_grad_body(g0, g1, g2, g3, f0, f1, f2, f3, own, p1, p2, p3, s0, s1, s2, s3, sems):
    copies = [
        pltpu.make_async_copy(source, target, sems.at[i])
        for i, (source, target) in enumerate(zip((f0, f1, f2, f3), (s0, s1, s2, s3)))
    ]
    for copy in copies:
        copy.start()
    for copy in copies:
        copy.wait()
    gates = jnp.concatenate([g0[...], g1[...], g2[...], g3[...]], axis=0)
    for by, out in ((2, p2), (1, p1), (3, p3), (0, own)):
        cut = slice(by * TOK, (by + 1) * TOK)
        left = jnp.concatenate([s0[:, cut], s1[:, cut], s2[:, cut], s3[:, cut]], axis=0)
        out[...] = dot(left, gates, (0, 0)).astype(out.dtype)


def choose_body(layers, feats, across_first, across_last, own):
    here = lax.axis_index("section")
    half = TOK // 2
    far = feats.at[lax.rem(layers[lax.rem(here + 2, 4)], 2)]
    across_first[...] = far[:half]
    across_last[...] = far[half:]
    own[...] = feats[lax.rem(layers[here], 2)]


def merge_body(layers, feats, from_left, from_right, to_next, to_back):
    here = lax.axis_index("section")
    half = TOK // 2
    for out, target, came, through in (
        (to_next, lax.rem(here + 1, 4), from_left, slice(0, half)),
        (to_back, lax.rem(here + 3, 4), from_right, slice(half, TOK)),
    ):
        layer = layers[target]
        out[...] = feats[lax.rem(layer, 2)]

        @pl.when(lax.div(layer, 2) != here)
        def _():
            out[through] = came[...]


def picked_body(layers, own, left, right, out):
    here = lax.axis_index("section")
    half = TOK // 2
    gap = lax.rem(lax.div(layers[here], 2) - here + 4, 4)

    @pl.when(gap == 0)
    def _():
        out[...] = own[...]

    @pl.when(gap == 1)
    def _():
        out[...] = right[...]

    @pl.when(gap == 2)
    def _():
        out[:half] = left[:half]
        out[half:] = right[half:]

    @pl.when(gap == 3)
    def _():
        out[...] = left[...]


def on_device(teacher_feats, layer_map, student_in, layer_weight, proj_weight, token_weight):
    section_count = lax.axis_size("section")
    m = lax.axis_index("mp")
    hidden = student_in[0]
    block = ((TOK, WIDE), bf16)
    wide = ((TOK, WIDE), f32)
    held = [pltpu.VMEM((4, TOK, WIDE), bf16)]

    half = ((TOK // 2, 2048), bf16)
    rows = ((TOK, 2048), bf16)
    mine = gather_z(layer_weight[0])
    across_first, across_last, own = call(choose_body, [half, half, rows], layer_map, teacher_feats, flops=2 * 10**10)
    from_left = shift(across_first, "section", 1)
    from_right = shift(across_last, "section", -1)
    to_next, to_back = call(merge_body, [rows, rows], layer_map, teacher_feats, from_left, from_right)
    left = shift(to_next, "section", 1)
    right = shift(to_back, "section", -1)
    start = after(hidden, to_next)
    hiddens = [hidden] + [shift(start, "mp", -d) for d in (1, 2, 3)]
    saved = call(
        saved_body, [block] * 4, *hiddens, scratch=[*held, pltpu.SemaphoreType.DMA((4, 4))], far_outs=1
    )
    weights = bring(after(proj_weight[0].reshape(4, WIDE, -1), to_back))
    own, weights = lax.optimization_barrier((own, weights))
    (picked,) = call(picked_body, [rows], layer_map, after(own, *hiddens), left, right)

    partial = []
    for d in (2, 1, 3, 0):
        part = lax.dynamic_index_in_dim(weights, (m + d) % 4, 0, keepdims=False)
        partial.append(jnp.einsum("te,ke->tk", picked, part, preferred_element_type=f32))
    own = partial[3]
    came = [shift(part.astype(bf16), "mp", d) for part, d in zip(partial, (2, 1, 3))]
    other_picked = cross(after(picked, own), 1)
    mine = after(mine, own, *came)
    theirs = cross(mine, 1)
    weight, act, slope = call(pre_body, [((4, WIDE, WIDE), bf16), wide, wide], *hiddens, mine, theirs, flops=3 * 10**8)
    saved = [saved[0]] + [cross(after(saved[x], own), x) for x in (1, 2, 3)]
    proj, sums = call(sums_body, [wide, ((8, TOK), f32)], own, *came, act)

    cgrad, qgrad, own, sgate, *parts = call(
        first_body,
        [wide, block, wide, block, block, block, block],
        after(sums, *saved, other_picked),
        *[shift(sums, "mp", d) for d in (2, 1, 3)],
        token_weight.reshape(1, TOK),
        act,
        proj,
        slope,
        weight,
        flops=3 * 10**8,
    )
    for step in range(section_count):
        if step > 0:
            own, sgate, *parts = call(
                step_body,
                [wide, block, block, block, block],
                incoming,
                cgrad,
                slope,
                weight,
                flops=3 * 10**8,
            )
        last = step + 1 == section_count
        if last:
            gates = [sgate, cross(sgate, 1), cross(sgate, 2)]
            gates.append(cross(gates[2], 1))
            layer_own, *layer_parts = call(
                layer_grad_body,
                [wide, block, block, block],
                *gates,
                *saved,
                flops=3 * 10**8,
                scratch=[pltpu.VMEM((TOK, WIDE), bf16)] * 4 + [pltpu.SemaphoreType.DMA((4,))],
                far=4,
            )
            parts = [after(part, layer_own) for part in parts]
        came = [shift(part, "mp", d) for part, d in zip(parts, (2, 1, 3))]
        result = (own + sum(x.astype(f32) for x in came)).astype(bf16)
        if not last:
            incoming = to_previous(result)
        if step == 0:
            start = after(qgrad, came[0])
            qgrads = [qgrad] + [shift(start, "mp", -d) for d in (1, 2, 3)]
            keep, give = call(split_body, [((TOK, 1024), bf16)] * 2, after(qgrads[0], incoming), *qgrads[1:], scratch=held)
            products = call(
                proj_grad_body,
                [((8 * TOK, 2048), bf16)],
                keep,
                cross(give, 1),
                picked,
                other_picked,
                limit=24,
            )
            grad_proj = sum_z(products[0])

    grad_proj = after(grad_proj, layer_own).astype(f32)
    layer_own, grad_proj = lax.optimization_barrier((layer_own, grad_proj))
    grad_layer = layer_own + sum(to_pair(part, d).astype(f32) for part, d in zip(layer_parts, (1, 2, 3)))
    grad_layer, own = lax.optimization_barrier((grad_layer, own))
    result = (own + sum(x.astype(f32) for x in came)).astype(bf16)
    return (result[None], grad_layer[None], grad_proj[None])


def solution(mesh):
    placed = (
        P("section", "dp", "mp"),
        P(),
        P("section", "dp", "mp"),
        P("section", "dp", "mp"),
        P("section", None, "mp"),
        P("dp"),
    )
    return jax.shard_map(
        on_device,
        mesh=mesh,
        in_specs=placed,
        out_specs=(P("section", "dp", "mp"), P("section", "dp", "mp"), P("section", "dp", "mp")),
        check_vma=False,
    )
```
